32 devices in a mesh: dp: 4 (over y, x), mp: 8 (over z, core).
Axes of the slice: x: 2, y: 2, z: 4, core: 2. Of those that a mesh axis runs over, the one named last changes fastest.
Arguments:
- inputs: bfloat16 [2048, 1024], P('dp'), may hold values from -60 to 60
- norm_gain_vector: float32 [1024], replicated, may hold values from 0.5 to 1.5
- query_saved: bfloat16 [2048, 16384], P('dp', 'mp'), may hold values from -5 to 5
- key_saved: bfloat16 [2048, 16384], P('dp', 'mp'), may hold values from -2 to 2
- value_saved: bfloat16 [2048, 16384], P('dp', 'mp'), may hold values from -6 to 6
- w_query: bfloat16 [1024, 16384], P(None, 'mp'), may hold values from -0.1875 to 0.1875
- w_key: bfloat16 [1024, 16384], P(None, 'mp'), may hold values from -0.1875 to 0.1875
- w_value: bfloat16 [1024, 16384], P(None, 'mp'), may hold values from -0.1875 to 0.1875
- w_out: bfloat16 [16384, 1024], P('mp'), may hold values from -0.046875 to 0.046875
- output_gradient: bfloat16 [2048, 1024], P('dp'), may hold values from -4 to 4
Outputs:
- grad_inputs: bfloat16 [2048, 1024], P('dp')
- grad_w_query: bfloat16 [1024, 16384], P(None, 'mp')
- grad_w_key: bfloat16 [1024, 16384], P(None, 'mp')
- grad_w_value: bfloat16 [1024, 16384], P(None, 'mp')
- grad_w_out: bfloat16 [16384, 1024], P('mp')
- grad_gain: float32 [1024], replicated
The draws below stay inside these ranges and needn't reach their ends.
All inputs are finite; a program needn't handle non-finite values.
Results may differ from the reference program's by a relative error of at most 0.034.
Values may be sent and summed in bfloat16 or wider, within the bound.
A program may use at most 128 MiB of HBM per device.

```python
import math
import jax
import jax.numpy as jnp
from jax import lax

D = 1024
HEADS = 128
HD = 128
SEQ = 512
INNER = 16384
TOKENS = 2048
N_DP = 4


def draw_inputs(key, part):
    first, second, third = jax.random.split(key, 3)
    base = jnp.clip(jax.random.normal(first, (TOKENS, D), jnp.float32), -6.0, 6.0)
    row_scale = jnp.exp(jax.random.uniform(second, (TOKENS, 1), jnp.float32, math.log(0.3), math.log(3.0)))
    col_scale = jnp.exp(jax.random.uniform(third, (1, D), jnp.float32, math.log(0.3), math.log(3.0)))
    return (base * row_scale * col_scale).astype(jnp.bfloat16)


def draw_pair(key):
    query_key = jax.random.fold_in(key, 101)
    key_key = jax.random.fold_in(key, 202)
    scale = HD ** (-0.5)
    queries = jnp.clip(jax.random.normal(query_key, (TOKENS, INNER), jnp.float32), -6.0, 6.0) * scale
    keys = jnp.clip(jax.random.normal(key_key, (TOKENS, INNER), jnp.float32), -6.0, 6.0) * scale
    return (queries.astype(jnp.bfloat16), keys.astype(jnp.bfloat16))


def draw_query_saved(key, part):
    return draw_pair(key)[0]


def draw_key_saved(key, part):
    return draw_pair(key)[1]


def steps_of(rng, extent, pieces, smallest, largest):
    def one(dim, parts):
        heights = jax.random.uniform(jax.random.fold_in(jax.random.fold_in(rng, 6), dim), (parts,), jnp.float32, smallest / len(pieces), largest / len(pieces))
        return jnp.repeat(jnp.exp(heights), extent[dim] // parts).reshape((-1,) + (1,) * (len(extent) - dim - 1))

    level = one(*pieces[0])
    for cut in pieces[1:]:
        level = level * one(*cut)
    return level


def gaussian(stream_key, shape, deviation, bound, shards=(), dtype=jnp.bfloat16):
    loudness = steps_of(stream_key, shape, shards, -0.22, 0.18) if shards else 1.0
    entries = jax.random.normal(stream_key, shape, jnp.float32) * deviation * loudness
    return jnp.minimum(jnp.maximum(entries, -bound), bound).astype(dtype)


def setup_inputs(seed: int = 0) -> dict:
    key_list = jax.random.split(jax.random.key(seed), 11)
    inputs = draw_inputs(jax.random.fold_in(key_list[10], 71), 0)
    norm_gain_vector = jnp.clip(1.0 + 0.1 * jax.random.normal(key_list[1], (D,), jnp.float32), 0.5, 1.5)
    query_saved = draw_query_saved(jax.random.fold_in(key_list[10], 71), 0)
    key_saved = draw_key_saved(jax.random.fold_in(key_list[10], 71), 0)
    value_saved = gaussian(key_list[4], (TOKENS, INNER), 1.0, 6.0, ((0, 4), (1, 8)))
    w_query = gaussian(key_list[5], (D, INNER), D ** -0.5, 0.1875, ((1, 8),))
    w_key = gaussian(key_list[6], (D, INNER), D ** -0.5, 0.1875, ((1, 8),))
    w_value = gaussian(key_list[7], (D, INNER), D ** -0.5, 0.1875, ((1, 8),))
    w_out = gaussian(key_list[8], (INNER, D), INNER ** -0.5, 0.046875, ((0, 8),))
    output_gradient = gaussian(key_list[9], (TOKENS, D), 0.25, 4.0, ((0, 4),))
    return dict(inputs=inputs, norm_gain_vector=norm_gain_vector, query_saved=query_saved, key_saved=key_saved, value_saved=value_saved, w_query=w_query, w_key=w_key, w_value=w_value, w_out=w_out, output_gradient=output_gradient)


def sequence_grads(block):
    rows, queries, keys_in, values, gradient_rows, gain_vector, w_query, w_key, w_value, w_out = block
    single_float_type = jnp.float32
    brain_float_half = jnp.bfloat16
    widened_rows = rows.astype(single_float_type)
    reciprocal_deviation = lax.rsqrt(lax.optimization_barrier(jnp.mean(widened_rows * widened_rows, axis=-1, keepdims=True)) + 1e-06)
    unit_input_rows = widened_rows * reciprocal_deviation
    normalized_rows = (unit_input_rows * gain_vector).astype(brain_float_half)
    query = queries.reshape(SEQ, HEADS, HD).astype(single_float_type)
    keys = keys_in.reshape(SEQ, HEADS, HD).astype(single_float_type)
    vals = values.reshape(SEQ, HEADS, HD).astype(single_float_type)
    scores = jnp.einsum('qhd,khd->hqk', query, keys)
    probs = jax.nn.softmax(scores, axis=-1)
    probs_low = probs.astype(brain_float_half)
    attended = jnp.einsum('hqk,khd->qhd', probs_low.astype(single_float_type), vals).astype(brain_float_half).reshape(SEQ, INNER)
    grad_att = jnp.dot(gradient_rows, w_out.T, preferred_element_type=single_float_type).astype(brain_float_half)
    part_out = jnp.dot(attended.T, gradient_rows, preferred_element_type=single_float_type)
    grad_att3 = grad_att.reshape(SEQ, HEADS, HD).astype(single_float_type)
    grad_val = jnp.einsum('hqk,qhd->khd', probs_low.astype(single_float_type), grad_att3).astype(brain_float_half)
    grad_prob = jnp.einsum('qhd,khd->hqk', grad_att3, vals)
    delta = lax.optimization_barrier(jnp.sum(probs * grad_prob, axis=-1, keepdims=True))
    grad_score = (probs * (grad_prob - delta)).astype(brain_float_half).astype(single_float_type)
    grad_query = jnp.einsum('hqk,khd->qhd', grad_score, keys).astype(brain_float_half).reshape(SEQ, INNER)
    grad_key = jnp.einsum('hqk,qhd->khd', grad_score, query).astype(brain_float_half).reshape(SEQ, INNER)
    grad_val = grad_val.reshape(SEQ, INNER)
    part_query = jnp.dot(normalized_rows.T, grad_query, preferred_element_type=single_float_type)
    part_key = jnp.dot(normalized_rows.T, grad_key, preferred_element_type=single_float_type)
    part_value = jnp.dot(normalized_rows.T, grad_val, preferred_element_type=single_float_type)
    normalized_gradient = jnp.dot(grad_query, w_query.T, preferred_element_type=single_float_type) + jnp.dot(grad_key, w_key.T, preferred_element_type=single_float_type) + jnp.dot(grad_val, w_value.T, preferred_element_type=single_float_type)
    scaled_gradient = normalized_gradient * gain_vector
    inner_product = lax.optimization_barrier(jnp.mean(scaled_gradient * unit_input_rows, axis=-1, keepdims=True))
    input_gradient = (gradient_rows.astype(single_float_type) + reciprocal_deviation * (scaled_gradient - unit_input_rows * inner_product)).astype(brain_float_half)
    partial_gain = lax.optimization_barrier(jnp.sum(normalized_gradient * unit_input_rows, axis=0))
    return (input_gradient, part_query.astype(brain_float_half), part_key.astype(brain_float_half), part_value.astype(brain_float_half), part_out.astype(brain_float_half), partial_gain.astype(brain_float_half))

def reference(inputs, norm_gain_vector, query_saved, key_saved, value_saved, w_query, w_key, w_value, w_out, output_gradient):

    def one(items):
        rows, queries, keys_in, values, gradient_rows = items
        return sequence_grads((rows, queries, keys_in, values, gradient_rows, norm_gain_vector, w_query, w_key, w_value, w_out))
    outs = lax.map(one, (inputs.reshape(N_DP, SEQ, D), query_saved.reshape(N_DP, SEQ, INNER), key_saved.reshape(N_DP, SEQ, INNER), value_saved.reshape(N_DP, SEQ, INNER), output_gradient.reshape(N_DP, SEQ, D)))
    grad_inputs = outs[0].reshape(TOKENS, D)
    grad_w_query = lax.optimization_barrier(jnp.sum(outs[1].astype(jnp.float32), axis=0)).astype(jnp.bfloat16)
    grad_w_key = lax.optimization_barrier(jnp.sum(outs[2].astype(jnp.float32), axis=0)).astype(jnp.bfloat16)
    grad_w_value = lax.optimization_barrier(jnp.sum(outs[3].astype(jnp.float32), axis=0)).astype(jnp.bfloat16)
    grad_w_out = lax.optimization_barrier(jnp.sum(outs[4].astype(jnp.float32), axis=0)).astype(jnp.bfloat16)
    grad_gain = lax.optimization_barrier(jnp.sum(outs[5].astype(jnp.float32), axis=0))
    return (grad_inputs, grad_w_query, grad_w_key, grad_w_value, grad_w_out, grad_gain)
```

```python
import jax
import jax.numpy as jnp
from jax import lax
from jax.experimental import pallas as pl
from jax.experimental.pallas import tpu as pltpu
from jax.sharding import PartitionSpec as P

HD = 128
N_DP = 4
MESH = pl.DeviceIdType.MESH
F32 = jnp.float32
BF16 = jnp.bfloat16


def norm_reverse_pass(
    gradient_rows, normalized_gradient, unit_input_rows, reciprocal_deviation, norm_gain_vector
):
    scaled_gradient = normalized_gradient * norm_gain_vector
    inner_product = jnp.mean(scaled_gradient * unit_input_rows, axis=-1, keepdims=True)
    input_gradient = gradient_rows.astype(jnp.float32) + reciprocal_deviation * (
        scaled_gradient - unit_input_rows * inner_product
    )
    return (input_gradient, jnp.sum(normalized_gradient * unit_input_rows, axis=0))


def shards(
    inputs,
    norm_gain_vector,
    query_saved,
    key_saved,
    value_saved,
    w_query,
    w_key,
    w_value,
    w_out,
    output_gradient,
):
    single_float_type = jnp.float32
    brain_float_half = jnp.bfloat16
    length = inputs.shape[0]
    width = query_saved.shape[1]
    heads = width // HD
    widened_rows = inputs.astype(single_float_type)
    reciprocal_deviation = lax.rsqrt(
        jnp.mean(widened_rows * widened_rows, axis=-1, keepdims=True) + 1e-06
    )
    unit_input_rows = widened_rows * reciprocal_deviation
    normalized_rows = (unit_input_rows * norm_gain_vector).astype(brain_float_half)
    query = query_saved.reshape(length, heads, HD)
    keys = key_saved.reshape(length, heads, HD)
    values = value_saved.reshape(length, heads, HD)
    scores = jnp.einsum("qhd,khd->hqk", query, keys, preferred_element_type=single_float_type)
    probs = jax.nn.softmax(scores, axis=-1)
    probs_low = probs.astype(brain_float_half)
    attended = (
        jnp.einsum("hqk,khd->qhd", probs_low, values, preferred_element_type=single_float_type)
        .astype(brain_float_half)
        .reshape(length, width)
    )
    grad_att = jnp.einsum(
        "td,id->ti", output_gradient, w_out, preferred_element_type=single_float_type
    ).astype(brain_float_half)
    part_out = jnp.einsum(
        "ti,td->id", attended, output_gradient, preferred_element_type=single_float_type
    )
    grad_att3 = grad_att.reshape(length, heads, HD)
    grad_val = (
        jnp.einsum("hqk,qhd->khd", probs_low, grad_att3, preferred_element_type=single_float_type)
        .astype(brain_float_half)
        .reshape(length, width)
    )
    grad_prob = jnp.einsum(
        "qhd,khd->hqk", grad_att3, values, preferred_element_type=single_float_type
    )
    delta = jnp.sum(probs * grad_prob, axis=-1, keepdims=True)
    grad_score = (probs * (grad_prob - delta)).astype(brain_float_half)
    grad_query = (
        jnp.einsum("hqk,khd->qhd", grad_score, keys, preferred_element_type=single_float_type)
        .astype(brain_float_half)
        .reshape(length, width)
    )
    grad_key = (
        jnp.einsum("hqk,qhd->khd", grad_score, query, preferred_element_type=single_float_type)
        .astype(brain_float_half)
        .reshape(length, width)
    )
    part_query = jnp.einsum(
        "td,ti->di", normalized_rows, grad_query, preferred_element_type=single_float_type
    )
    part_key = jnp.einsum(
        "td,ti->di", normalized_rows, grad_key, preferred_element_type=single_float_type
    )
    part_value = jnp.einsum(
        "td,ti->di", normalized_rows, grad_val, preferred_element_type=single_float_type
    )
    total = jnp.einsum("ti,di->td", grad_query, w_query, preferred_element_type=single_float_type)
    total = total + jnp.einsum(
        "ti,di->td", grad_key, w_key, preferred_element_type=single_float_type
    )
    normalized_gradient = lax.psum(
        (
            total
            + jnp.einsum("ti,di->td", grad_val, w_value, preferred_element_type=single_float_type)
        ).astype(jnp.bfloat16),
        "mp",
    ).astype(jnp.float32)
    input_gradient, partial_gain = norm_reverse_pass(
        output_gradient,
        normalized_gradient,
        unit_input_rows,
        reciprocal_deviation,
        norm_gain_vector,
    )
    grad_inputs = input_gradient.astype(brain_float_half)
    sum_query, sum_key, sum_value, sum_out, sum_gain = (
        lax.psum(part_query.astype(jnp.bfloat16), "dp").astype(jnp.float32),
        lax.psum(part_key.astype(jnp.bfloat16), "dp").astype(jnp.float32),
        lax.psum(part_value.astype(jnp.bfloat16), "dp").astype(jnp.float32),
        lax.psum(part_out.astype(jnp.bfloat16), "dp").astype(jnp.float32),
        lax.psum(partial_gain.astype(jnp.bfloat16), "dp").astype(jnp.float32),
    )
    return (
        grad_inputs,
        sum_query.astype(brain_float_half),
        sum_key.astype(brain_float_half),
        sum_value.astype(brain_float_half),
        sum_out.astype(brain_float_half),
        sum_gain,
    )


def dot_nn(a, b):
    return lax.dot_general(a, b, (((1,), (0,)), ((), ())), preferred_element_type=F32)


def dot_nt(a, b):
    return lax.dot_general(a, b, (((1,), (1,)), ((), ())), preferred_element_type=F32)


def dot_tn(a, b):
    return lax.dot_general(a, b, (((0,), (0,)), ((), ())), preferred_element_type=F32)


def flipped(me, mask):
    x, y = me % 2, me // 2
    bx, by = mask % 2, mask // 2
    return (y + by * (1 - 2 * y)) * 2 + x + bx * (1 - 2 * x)


def greet(partners):
    barrier = pltpu.get_barrier_semaphore()
    for partner in partners:
        pl.semaphore_signal(barrier, inc=1, device_id=partner, device_id_type=MESH)
    pl.semaphore_wait(barrier, len(partners))


def attention_kernel(
    q_ref, k_ref, v_ref, wq_ref, wk_ref, wv_ref, wo_ref, rows_ref,
    grads_out, att_out, gathered_out, total_out,
    grads_buf, att_buf, total,
    a2a_send, a2a_recv, gather_send, gather_recv, local_sem,
):
    me, mp = lax.axis_index("dp"), lax.axis_index("mp")
    core, half = mp % 2, (mp // 2) % 2
    other_core = (me, mp + 1 - 2 * core)
    other_z = (me, mp + 2 - 4 * half)
    greet([(flipped(me, 1), mp), (flipped(me, 2), mp), (flipped(me, 3), mp), other_core, other_z])
    depth = rows_ref.shape[1] // 2
    steps = grads_buf.shape[0]

    def gather_copy(slot, src, array, owner, part, target):
        rows = pl.ds(pl.multiple_of(part * depth, depth), depth)
        return pltpu.make_async_remote_copy(
            src_ref=src.at[array, rows] if src is rows_ref else src.at[array, owner, rows],
            dst_ref=gathered_out.at[array, owner, rows],
            send_sem=gather_send.at[slot],
            recv_sem=gather_recv.at[slot],
            device_id=target,
            device_id_type=MESH,
        )

    def spread(mask):
        return gather_copy(mask - 1, rows_ref, core, me, half, (flipped(me, mask), mp))

    def along_z(mask):
        return gather_copy(2 + mask, gathered_out, core, flipped(me, mask), half, other_z)

    def across(mask, second):
        part = 1 - half if second else half
        return gather_copy(
            5 + mask + 3 * second, gathered_out, core, flipped(me, mask), part, other_core
        )

    def own_rows(array):
        return pltpu.make_async_copy(
            rows_ref.at[array], gathered_out.at[array, me], local_sem.at[array]
        )

    for mask in (1, 2, 3):
        spread(mask).start()
    own_rows(0).start()
    own_rows(1).start()

    def place(step):
        return step // N_DP, flipped(me, (step % N_DP + 1) % N_DP)

    def remote(step):
        k, target = place(step)
        return [
            pltpu.make_async_remote_copy(
                src_ref=buf.at[step],
                dst_ref=out.at[k, me],
                send_sem=a2a_send.at[i, step],
                recv_sem=a2a_recv.at[i, step],
                device_id=(target, mp),
                device_id_type=MESH,
            )
            for i, (buf, out) in enumerate(((grads_buf, grads_out), (att_buf, att_out)))
        ]

    def local(step):
        k, _ = place(step)
        return [
            pltpu.make_async_copy(buf.at[step], out.at[k, me], a2a_send.at[i, step])
            for i, (buf, out) in enumerate(((grads_buf, grads_out), (att_buf, att_out)))
        ]

    total[...] = jnp.zeros_like(total)
    per_chunk = steps // N_DP

    def head_step(step, carry):
        k, target = place(step)
        cols = pl.ds(pl.multiple_of((target * per_chunk + k) * HD, HD), HD)
        query, keys, values = q_ref[:, cols], k_ref[:, cols], v_ref[:, cols]
        grad_att = dot_nn(wo_ref[cols, :], rows_ref[1]).astype(BF16)
        scores = dot_nt(keys, query)
        weights = jnp.exp(scores - jnp.max(scores, axis=0, keepdims=True))
        probs = weights * (1.0 / jnp.sum(weights, axis=0, keepdims=True))
        probs_low = probs.astype(BF16)
        att_buf[step] = dot_tn(values, probs_low).astype(BF16)
        grad_val = dot_nt(probs_low, grad_att).astype(BF16)
        grad_prob = dot_nn(values, grad_att)
        delta = jnp.sum(probs * grad_prob, axis=0, keepdims=True)
        grad_score = (probs * (grad_prob - delta)).astype(BF16)
        grad_query = jnp.transpose(dot_tn(keys, grad_score)).astype(BF16)
        grad_key = dot_nn(grad_score, query).astype(BF16)
        grads = jnp.concatenate([grad_query, grad_key, grad_val], axis=1)
        grads_buf[step] = grads

        @pl.when(step % N_DP != N_DP - 1)
        def _():
            for copy in remote(step):
                copy.start()

        @pl.when(step % N_DP == N_DP - 1)
        def _():
            for copy in local(step):
                copy.start()

        projections = jnp.concatenate([wq_ref[:, cols], wk_ref[:, cols], wv_ref[:, cols]], axis=1)
        total[...] += dot_nt(grads, projections)
        return carry

    lax.fori_loop(0, steps // 2, head_step, 0)
    for mask in (1, 2, 3):
        spread(mask).wait_recv()
        along_z(mask).start()
        across(mask, 0).start()
    lax.fori_loop(steps // 2, steps, head_step, 0)
    total_out[...] = total[...].astype(BF16)
    for mask in (1, 2, 3):
        along_z(mask).wait_recv()
        across(mask, 1).start()

    def drain(step, carry):
        @pl.when(step % N_DP != N_DP - 1)
        def _():
            for copy in remote(step):
                copy.wait()

        @pl.when(step % N_DP == N_DP - 1)
        def _():
            for copy in local(step):
                copy.wait()

        return carry

    lax.fori_loop(0, steps, drain, 0)
    for mask in (1, 2, 3):
        spread(mask).wait_send()
        along_z(mask).wait_send()
        across(mask, 0).wait()
        across(mask, 1).wait()
    own_rows(0).wait()
    own_rows(1).wait()


def weight_kernel(
    grads_ref, att_ref, gathered_ref,
    gq_out, gk_out, gv_out, go_out,
    wide, tall,
    send_sem, recv_sem, local_sem,
):
    me, mp = lax.axis_index("dp"), lax.axis_index("mp")
    peer_x, peer_y = flipped(me, 1), flipped(me, 2)
    greet([(peer_x, mp), (peer_y, mp)])
    per_chunk = grads_ref.shape[0]
    pieces = wide.shape[1]
    height, width = wide.shape[2], wide.shape[3]
    outs = (gq_out, gk_out, gv_out, go_out)

    def spot(array, piece, owner, part=None):
        if array < 3:
            first, size = piece * height, height
            cols = pl.ds(pl.multiple_of(owner * width, width), width)
        else:
            first, size = (owner * per_chunk + piece) * HD, HD
            cols = slice(None)
        if part is not None:
            size = size // 2
            first = first + part * size
        return outs[array].at[pl.ds(pl.multiple_of(first, size), size), cols]

    def staged(array, piece):
        return wide.at[array, piece] if array < 3 else tall.at[piece]

    def copy_to(kind, array, piece, src, dst, peer):
        return pltpu.make_async_remote_copy(
            src_ref=src,
            dst_ref=dst,
            send_sem=send_sem.at[kind, array, piece],
            recv_sem=recv_sem.at[kind, array, piece],
            device_id=(peer, mp),
            device_id_type=MESH,
        )

    def own(kind, array, piece):
        return copy_to(
            kind, array, piece, staged(array, piece), spot(array, piece, me), (peer_x, peer_y)[kind]
        )

    def forward(kind, array, piece):
        block = spot(array, piece, (peer_x, peer_y)[kind], kind)
        return copy_to(2 + kind, array, piece, block, block, (peer_y, peer_x)[kind])

    def keep(array, piece):
        return pltpu.make_async_copy(
            staged(array, piece), spot(array, piece, me), local_sem.at[array, piece]
        )

    def send(array, piece):
        own(0, array, piece).start()
        own(1, array, piece).start()
        keep(array, piece).start()

    for array in range(3):
        lanes = slice(array * HD, (array + 1) * HD)

        def wide_step(piece, carry, array=array, lanes=lanes):
            rows = pl.ds(pl.multiple_of(piece * height, height), height)
            acc = None
            for owner in range(N_DP):
                right = jnp.concatenate(
                    [grads_ref[k, owner, :, lanes] for k in range(per_chunk)], axis=1
                )
                term = dot_nn(gathered_ref[0, owner, rows, :], right)
                acc = term if acc is None else acc + term
            wide[array, piece] = acc.astype(BF16)
            send(array, piece)
            return carry

        lax.fori_loop(0, pieces, wide_step, 0)

    def tall_step(piece, carry):
        acc = None
        for owner in range(N_DP):
            term = dot_nt(att_ref[piece, owner], gathered_ref[1, owner])
            acc = term if acc is None else acc + term
        tall[piece] = acc.astype(BF16)
        send(3, piece)
        return carry

    lax.fori_loop(0, per_chunk, tall_step, 0)

    def count(array):
        return pieces if array < 3 else per_chunk

    for array in range(4):

        def pass_on(piece, carry, array=array):
            for kind in (0, 1):
                own(kind, array, piece).wait_recv()
                forward(kind, array, piece).start()
            return carry

        lax.fori_loop(0, count(array), pass_on, 0)
    for array in range(4):

        def finish(piece, carry, array=array):
            for kind in (0, 1):
                own(kind, array, piece).wait_send()
                forward(kind, array, piece).wait()
            keep(array, piece).wait()
            return carry

        lax.fori_loop(0, count(array), finish, 0)


def fused_grads(
    normalized_rows, query_saved, key_saved, value_saved, w_query, w_key, w_value, w_out, output_gradient
):
    length, width = query_saved.shape
    features = normalized_rows.shape[1]
    steps = width // HD
    per_chunk = steps // N_DP
    rows = jnp.stack([normalized_rows.T, output_gradient.T])
    vmem, hbm = pl.BlockSpec(memory_space=pltpu.VMEM), pl.BlockSpec(memory_space=pl.ANY)
    dma = pltpu.SemaphoreType.DMA
    grads, att, gathered, total = pl.pallas_call(
        attention_kernel,
        out_shape=(
            jax.ShapeDtypeStruct((per_chunk, N_DP, length, 3 * HD), BF16),
            jax.ShapeDtypeStruct((per_chunk, N_DP, HD, length), BF16),
            jax.ShapeDtypeStruct((2, N_DP, features, length), BF16),
            jax.ShapeDtypeStruct((length, features), BF16),
        ),
        in_specs=[vmem] * 8,
        out_specs=(hbm, hbm, hbm, vmem),
        scratch_shapes=[
            pltpu.VMEM((steps, length, 3 * HD), BF16),
            pltpu.VMEM((steps, HD, length), BF16),
            pltpu.VMEM((length, features), F32),
            dma((2, steps)),
            dma((2, steps)),
            dma((12,)),
            dma((12,)),
            dma((2,)),
        ],
        compiler_params=pltpu.CompilerParams(
            collective_id=0, has_side_effects=True, vmem_limit_bytes=56 * 2**20
        ),
        cost_estimate=pl.CostEstimate(
            flops=30 * length * width * features, bytes_accessed=40 * 2**20, transcendentals=0
        ),
    )(query_saved, key_saved, value_saved, w_query, w_key, w_value, w_out, rows)
    pieces = 4
    outs = pl.pallas_call(
        weight_kernel,
        out_shape=(jax.ShapeDtypeStruct((features, width), BF16),) * 3
        + (jax.ShapeDtypeStruct((width, features), BF16),),
        in_specs=[vmem] * 3,
        out_specs=(hbm,) * 4,
        scratch_shapes=[
            pltpu.VMEM((3, pieces, features // pieces, per_chunk * HD), BF16),
            pltpu.VMEM((per_chunk, HD, features), BF16),
            dma((4, 4, max(pieces, per_chunk))),
            dma((4, 4, max(pieces, per_chunk))),
            dma((4, max(pieces, per_chunk))),
        ],
        compiler_params=pltpu.CompilerParams(
            collective_id=1, has_side_effects=True, vmem_limit_bytes=48 * 2**20
        ),
        cost_estimate=pl.CostEstimate(
            flops=200 * length * width * features, bytes_accessed=200 * 2**20, transcendentals=0
        ),
    )(grads, att, gathered)
    return total, outs


def fused_shards(
    inputs,
    norm_gain_vector,
    query_saved,
    key_saved,
    value_saved,
    w_query,
    w_key,
    w_value,
    w_out,
    output_gradient,
):
    widened_rows = inputs.astype(F32)
    reciprocal_deviation = lax.rsqrt(
        jnp.mean(widened_rows * widened_rows, axis=-1, keepdims=True) + 1e-06
    )
    unit_input_rows = widened_rows * reciprocal_deviation
    normalized_rows = (unit_input_rows * norm_gain_vector).astype(BF16)
    total, outs = fused_grads(
        normalized_rows, query_saved, key_saved, value_saved, w_query, w_key, w_value, w_out,
        output_gradient,
    )
    normalized_gradient = lax.psum(total, "mp").astype(F32)
    input_gradient, partial_gain = norm_reverse_pass(
        output_gradient,
        normalized_gradient,
        unit_input_rows,
        reciprocal_deviation,
        norm_gain_vector,
    )
    sum_gain = lax.psum(partial_gain.astype(BF16), "dp").astype(F32)
    return (input_gradient.astype(BF16), *outs, sum_gain)


def fits(mesh, arguments):
    length, width = arguments[2].shape
    n_dp, n_mp = mesh.shape["dp"], mesh.shape["mp"]
    return (
        n_dp == N_DP
        and n_mp % 4 == 0
        and width % (n_mp * N_DP * HD) == 0
        and width <= 2048 * n_mp
        and length == 512 * n_dp
        and arguments[0].shape[1] == 1024
    )


def solution(mesh):
    def whole(*arguments):
        return jax.shard_map(
            fused_shards if fits(mesh, arguments) else shards,
            mesh=mesh,
            in_specs=(
                P("dp", None),
                P(),
                P("dp", "mp"),
                P("dp", "mp"),
                P("dp", "mp"),
                P(None, "mp"),
                P(None, "mp"),
                P(None, "mp"),
                P("mp", None),
                P("dp", None),
            ),
            out_specs=(
                P("dp", None), P(None, "mp"), P(None, "mp"), P(None, "mp"), P("mp", None), P(),
            ),
            check_vma=False,
        )(*arguments)

    return whole
```

```python
import functools

import jax
import jax.numpy as jnp
from jax import lax
from jax.experimental import pallas as pl
from jax.experimental.pallas import tpu as pltpu
from jax.sharding import PartitionSpec as P

HD = 128
N_DP = 4
MESH = pl.DeviceIdType.MESH
F32 = jnp.float32
BF16 = jnp.bfloat16


def norm_reverse_pass(
    gradient_rows, normalized_gradient, unit_input_rows, reciprocal_deviation, norm_gain_vector
):
    scaled_gradient = normalized_gradient * norm_gain_vector
    inner_product = jnp.mean(scaled_gradient * unit_input_rows, axis=-1, keepdims=True)
    input_gradient = gradient_rows.astype(jnp.float32) + reciprocal_deviation * (
        scaled_gradient - unit_input_rows * inner_product
    )
    return (input_gradient, jnp.sum(normalized_gradient * unit_input_rows, axis=0))


def shards(
    inputs,
    norm_gain_vector,
    query_saved,
    key_saved,
    value_saved,
    w_query,
    w_key,
    w_value,
    w_out,
    output_gradient,
):
    single_float_type = jnp.float32
    brain_float_half = jnp.bfloat16
    length = inputs.shape[0]
    width = query_saved.shape[1]
    heads = width // HD
    widened_rows = inputs.astype(single_float_type)
    reciprocal_deviation = lax.rsqrt(
        jnp.mean(widened_rows * widened_rows, axis=-1, keepdims=True) + 1e-06
    )
    unit_input_rows = widened_rows * reciprocal_deviation
    normalized_rows = (unit_input_rows * norm_gain_vector).astype(brain_float_half)
    query = query_saved.reshape(length, heads, HD)
    keys = key_saved.reshape(length, heads, HD)
    values = value_saved.reshape(length, heads, HD)
    scores = jnp.einsum("qhd,khd->hqk", query, keys, preferred_element_type=single_float_type)
    probs = jax.nn.softmax(scores, axis=-1)
    probs_low = probs.astype(brain_float_half)
    attended = (
        jnp.einsum("hqk,khd->qhd", probs_low, values, preferred_element_type=single_float_type)
        .astype(brain_float_half)
        .reshape(length, width)
    )
    grad_att = jnp.einsum(
        "td,id->ti", output_gradient, w_out, preferred_element_type=single_float_type
    ).astype(brain_float_half)
    part_out = jnp.einsum(
        "ti,td->id", attended, output_gradient, preferred_element_type=single_float_type
    )
    grad_att3 = grad_att.reshape(length, heads, HD)
    grad_val = (
        jnp.einsum("hqk,qhd->khd", probs_low, grad_att3, preferred_element_type=single_float_type)
        .astype(brain_float_half)
        .reshape(length, width)
    )
    grad_prob = jnp.einsum(
        "qhd,khd->hqk", grad_att3, values, preferred_element_type=single_float_type
    )
    delta = jnp.sum(probs * grad_prob, axis=-1, keepdims=True)
    grad_score = (probs * (grad_prob - delta)).astype(brain_float_half)
    grad_query = (
        jnp.einsum("hqk,khd->qhd", grad_score, keys, preferred_element_type=single_float_type)
        .astype(brain_float_half)
        .reshape(length, width)
    )
    grad_key = (
        jnp.einsum("hqk,qhd->khd", grad_score, query, preferred_element_type=single_float_type)
        .astype(brain_float_half)
        .reshape(length, width)
    )
    part_query = jnp.einsum(
        "td,ti->di", normalized_rows, grad_query, preferred_element_type=single_float_type
    )
    part_key = jnp.einsum(
        "td,ti->di", normalized_rows, grad_key, preferred_element_type=single_float_type
    )
    part_value = jnp.einsum(
        "td,ti->di", normalized_rows, grad_val, preferred_element_type=single_float_type
    )
    total = jnp.einsum("ti,di->td", grad_query, w_query, preferred_element_type=single_float_type)
    total = total + jnp.einsum(
        "ti,di->td", grad_key, w_key, preferred_element_type=single_float_type
    )
    normalized_gradient = lax.psum(
        (
            total
            + jnp.einsum("ti,di->td", grad_val, w_value, preferred_element_type=single_float_type)
        ).astype(jnp.bfloat16),
        "mp",
    ).astype(jnp.float32)
    input_gradient, partial_gain = norm_reverse_pass(
        output_gradient,
        normalized_gradient,
        unit_input_rows,
        reciprocal_deviation,
        norm_gain_vector,
    )
    grad_inputs = input_gradient.astype(brain_float_half)
    sum_query, sum_key, sum_value, sum_out, sum_gain = (
        lax.psum(part_query.astype(jnp.bfloat16), "dp").astype(jnp.float32),
        lax.psum(part_key.astype(jnp.bfloat16), "dp").astype(jnp.float32),
        lax.psum(part_value.astype(jnp.bfloat16), "dp").astype(jnp.float32),
        lax.psum(part_out.astype(jnp.bfloat16), "dp").astype(jnp.float32),
        lax.psum(partial_gain.astype(jnp.bfloat16), "dp").astype(jnp.float32),
    )
    return (
        grad_inputs,
        sum_query.astype(brain_float_half),
        sum_key.astype(brain_float_half),
        sum_value.astype(brain_float_half),
        sum_out.astype(brain_float_half),
        sum_gain,
    )


def dot_nn(a, b):
    return lax.dot_general(a, b, (((1,), (0,)), ((), ())), preferred_element_type=F32)


def dot_nt(a, b):
    return lax.dot_general(a, b, (((1,), (1,)), ((), ())), preferred_element_type=F32)


def dot_tn(a, b):
    return lax.dot_general(a, b, (((0,), (0,)), ((), ())), preferred_element_type=F32)


def flipped(me, mask):
    x, y = me % 2, me // 2
    bx, by = mask % 2, mask // 2
    return (y + by * (1 - 2 * y)) * 2 + x + bx * (1 - 2 * x)


def greet(partners):
    barrier = pltpu.get_barrier_semaphore()
    for partner in partners:
        pl.semaphore_signal(barrier, inc=1, device_id=partner, device_id_type=MESH)
    pl.semaphore_wait(barrier, len(partners))


def attention_kernel(
    n_mp,
    q_hbm, k_hbm, v_hbm, wq_hbm, wk_hbm, wv_hbm, wo_hbm, rows_ref,
    grads_out, att_out, gathered_out, total_out,
    q_ref, k_ref, v_ref, wq_ref, wk_ref, wv_ref, wo_ref,
    grads_buf, att_buf, total,
    a2a_send, a2a_recv, gather_send, gather_recv, local_sem, load_sem,
):
    me, mp = lax.axis_index("dp"), lax.axis_index("mp")
    parts = n_mp // 2
    core, z = mp % 2, mp // 2
    other_core = (me, mp + 1 - 2 * core)
    loads = [
        pltpu.make_async_copy(src, dst, load_sem.at[i])
        for i, (src, dst) in enumerate(
            (
                (q_hbm, q_ref), (k_hbm, k_ref), (v_hbm, v_ref), (wo_hbm, wo_ref),
                (wq_hbm, wq_ref), (wk_hbm, wk_ref), (wv_hbm, wv_ref),
            )
        )
    ]
    for load in loads:
        load.start()

    def along(j):
        return (me, (z + j) % parts * 2 + core)

    greet(
        [(flipped(me, mask), mp) for mask in (1, 2, 3)]
        + [other_core]
        + [along(j) for j in range(1, parts)]
    )
    depth = rows_ref.shape[1] // parts
    steps = grads_buf.shape[0]

    def gather_copy(slot, src, array, owner, part, target):
        rows = pl.ds(pl.multiple_of(part * depth, depth), depth)
        return pltpu.make_async_remote_copy(
            src_ref=src.at[array, rows] if src is rows_ref else src.at[array, owner, rows],
            dst_ref=gathered_out.at[array, owner, rows],
            send_sem=gather_send.at[slot],
            recv_sem=gather_recv.at[slot],
            device_id=target,
            device_id_type=MESH,
        )

    def spread(mask):
        return gather_copy(mask - 1, rows_ref, core, me, z, (flipped(me, mask), mp))

    def along_z(mask, j):
        return gather_copy(
            3 * j + mask - 1, gathered_out, core, flipped(me, mask), z, along(j)
        )

    def across(mask, j):
        return gather_copy(
            3 * (parts + j) + mask - 1, gathered_out, core, flipped(me, mask),
            (z - j + parts) % parts, other_core,
        )

    def own_rows(array):
        return pltpu.make_async_copy(
            rows_ref.at[array], gathered_out.at[array, me], local_sem.at[array]
        )

    for mask in (1, 2, 3):
        spread(mask).start()
    own_rows(0).start()
    own_rows(1).start()

    def place(step):
        return step // N_DP, flipped(me, (step % N_DP + 1) % N_DP)

    def remote(step):
        k, target = place(step)
        return [
            pltpu.make_async_remote_copy(
                src_ref=buf.at[step],
                dst_ref=out.at[k, me],
                send_sem=a2a_send.at[i, step],
                recv_sem=a2a_recv.at[i, step],
                device_id=(target, mp),
                device_id_type=MESH,
            )
            for i, (buf, out) in enumerate(((grads_buf, grads_out), (att_buf, att_out)))
        ]

    def local(step):
        k, _ = place(step)
        return [
            pltpu.make_async_copy(buf.at[step], out.at[k, me], a2a_send.at[i, step])
            for i, (buf, out) in enumerate(((grads_buf, grads_out), (att_buf, att_out)))
        ]

    total[...] = jnp.zeros_like(total)
    for load in loads[:4]:
        load.wait()
    per_chunk = steps // N_DP

    def head_step(step, carry):
        k, target = place(step)
        cols = pl.ds(pl.multiple_of((target * per_chunk + k) * HD, HD), HD)
        query, keys, values = q_ref[:, cols], k_ref[:, cols], v_ref[:, cols]
        grad_att = dot_nn(wo_ref[cols, :], rows_ref[1]).astype(BF16)
        scores = dot_nt(keys, query)
        weights = jnp.exp(scores - jnp.max(scores, axis=0, keepdims=True))
        probs = weights * (1.0 / jnp.sum(weights, axis=0, keepdims=True))
        probs_low = probs.astype(BF16)
        att_buf[step] = dot_tn(values, probs_low).astype(BF16)
        grad_val = dot_nt(probs_low, grad_att).astype(BF16)
        grad_prob = dot_nn(values, grad_att)
        delta = jnp.sum(probs * grad_prob, axis=0, keepdims=True)
        grad_score = (probs * (grad_prob - delta)).astype(BF16)
        grad_query = jnp.transpose(dot_tn(keys, grad_score)).astype(BF16)
        grad_key = dot_nn(grad_score, query).astype(BF16)
        grads = jnp.concatenate([grad_query, grad_key, grad_val], axis=1)
        grads_buf[step] = grads

        @pl.when(step % N_DP != N_DP - 1)
        def _():
            for copy in remote(step):
                copy.start()

        @pl.when(step % N_DP == N_DP - 1)
        def _():
            for copy in local(step):
                copy.start()

        @pl.when(step == 0)
        def _():
            for load in loads[4:]:
                load.wait()

        projections = jnp.concatenate([wq_ref[:, cols], wk_ref[:, cols], wv_ref[:, cols]], axis=1)
        total[...] += dot_nt(grads, projections)
        return carry

    lax.fori_loop(0, N_DP, head_step, 0)
    for mask in (1, 2, 3):
        spread(mask).wait_recv()
        for j in range(1, parts):
            along_z(mask, j).start()
        across(mask, 0).start()
    lax.fori_loop(N_DP, steps, head_step, 0)
    total_out[...] = total[...].astype(BF16)
    for j in range(1, parts):
        for mask in (1, 2, 3):
            along_z(mask, j).wait_recv()
            across(mask, j).start()

    def drain(step, carry):
        @pl.when(step % N_DP != N_DP - 1)
        def _():
            for copy in remote(step):
                copy.wait()

        @pl.when(step % N_DP == N_DP - 1)
        def _():
            for copy in local(step):
                copy.wait()

        return carry

    lax.fori_loop(0, steps, drain, 0)
    for mask in (1, 2, 3):
        spread(mask).wait_send()
        for j in range(1, parts):
            along_z(mask, j).wait_send()
        for j in range(parts):
            across(mask, j).wait()
    own_rows(0).wait()
    own_rows(1).wait()


def weight_kernel(
    n_mp,
    grads_ref, att_hbm, gathered_hbm, total_ref, inputs_ref, outgrad_ref, gain_ref,
    gq_out, gk_out, gv_out, go_out, gi_out, gain_out,
    att_ref, gathered_ref, wide, tall, landing, gi_buf, gain_slots, gain_seqs,
    send_sem, recv_sem, local_sem, load_sem,
    total_send, total_recv, gi_send, gi_recv, slot_send, slot_recv, seq_send, seq_recv,
):
    me, mp = lax.axis_index("dp"), lax.axis_index("mp")
    peer_x, peer_y = flipped(me, 1), flipped(me, 2)
    loads = [
        pltpu.make_async_copy(gathered_hbm.at[0], gathered_ref.at[0], load_sem.at[0]),
        pltpu.make_async_copy(att_hbm, att_ref, load_sem.at[1]),
        pltpu.make_async_copy(gathered_hbm.at[1], gathered_ref.at[1], load_sem.at[2]),
    ]
    for load in loads:
        load.start()

    def ahead(i):
        return (mp + i) % n_mp

    greet(
        [(flipped(me, mask), mp) for mask in (1, 2, 3)] + [(me, ahead(i)) for i in range(1, n_mp)]
    )
    share = total_ref.shape[0] // n_mp

    def rows_of(index):
        return pl.ds(pl.multiple_of(index * share, share), share)

    def total_copy(i):
        return pltpu.make_async_remote_copy(
            src_ref=total_ref.at[rows_of(ahead(i))],
            dst_ref=landing.at[i],
            send_sem=total_send.at[i],
            recv_sem=total_recv.at[i],
            device_id=(me, ahead(i)),
            device_id_type=MESH,
        )

    def gi_copy(i):
        return pltpu.make_async_remote_copy(
            src_ref=gi_buf,
            dst_ref=gi_out.at[rows_of(mp)],
            send_sem=gi_send.at[i],
            recv_sem=gi_recv.at[i],
            device_id=(me, ahead(i)),
            device_id_type=MESH,
        )

    def slot_copy(i):
        return pltpu.make_async_remote_copy(
            src_ref=gain_slots.at[mp],
            dst_ref=gain_slots.at[mp],
            send_sem=slot_send.at[i],
            recv_sem=slot_recv.at[i],
            device_id=(me, ahead(i)),
            device_id_type=MESH,
        )

    def seq_copy(mask):
        return pltpu.make_async_remote_copy(
            src_ref=gain_seqs.at[me],
            dst_ref=gain_seqs.at[me],
            send_sem=seq_send.at[mask],
            recv_sem=seq_recv.at[mask],
            device_id=(flipped(me, mask), mp),
            device_id_type=MESH,
        )

    gi_keep = pltpu.make_async_copy(gi_buf, gi_out.at[rows_of(mp)], gi_send.at[0])
    others = range(1, n_mp)
    for i in others:
        total_copy(i).start()
    per_chunk = grads_ref.shape[0]
    pieces = wide.shape[1]
    height, width = wide.shape[2], wide.shape[3]
    outs = (gq_out, gk_out, gv_out, go_out)

    def spot(array, piece, owner, part=None):
        if array < 3:
            first, size = piece * height, height
            cols = pl.ds(pl.multiple_of(owner * width, width), width)
        else:
            first, size = (owner * per_chunk + piece) * HD, HD
            cols = slice(None)
        if part is not None:
            size = size // 2
            first = first + part * size
        return outs[array].at[pl.ds(pl.multiple_of(first, size), size), cols]

    def staged(array, piece):
        return wide.at[array, piece] if array < 3 else tall.at[piece]

    def copy_to(kind, array, piece, src, dst, peer):
        return pltpu.make_async_remote_copy(
            src_ref=src,
            dst_ref=dst,
            send_sem=send_sem.at[kind, array, piece],
            recv_sem=recv_sem.at[kind, array, piece],
            device_id=(peer, mp),
            device_id_type=MESH,
        )

    def own(kind, array, piece):
        return copy_to(
            kind, array, piece, staged(array, piece), spot(array, piece, me), (peer_x, peer_y)[kind]
        )

    def forward(kind, array, piece):
        block = spot(array, piece, (peer_x, peer_y)[kind], kind)
        return copy_to(2 + kind, array, piece, block, block, (peer_y, peer_x)[kind])

    def keep(array, piece):
        return pltpu.make_async_copy(
            staged(array, piece), spot(array, piece, me), local_sem.at[array, piece]
        )

    def send(array, piece):
        own(0, array, piece).start()
        own(1, array, piece).start()
        keep(array, piece).start()

    loads[0].wait()
    for array in range(3):
        lanes = slice(array * HD, (array + 1) * HD)

        def wide_step(piece, carry, array=array, lanes=lanes):
            rows = pl.ds(pl.multiple_of(piece * height, height), height)
            acc = None
            for owner in range(N_DP):
                right = jnp.concatenate(
                    [grads_ref[k, owner, :, lanes] for k in range(per_chunk)], axis=1
                )
                term = dot_nn(gathered_ref[0, owner, rows, :], right)
                acc = term if acc is None else acc + term
            wide[array, piece] = acc.astype(BF16)
            send(array, piece)
            return carry

        lax.fori_loop(0, pieces, wide_step, 0)

    loads[1].wait()
    loads[2].wait()

    def tall_step(piece, carry):
        acc = None
        for owner in range(N_DP):
            term = dot_nt(att_ref[piece, owner], gathered_ref[1, owner])
            acc = term if acc is None else acc + term
        tall[piece] = acc.astype(BF16)
        send(3, piece)
        return carry

    lax.fori_loop(0, per_chunk, tall_step, 0)

    normed_grad = total_ref[rows_of(mp), :].astype(F32)
    for i in others:
        total_copy(i).wait_recv()
        normed_grad += landing[i].astype(F32)
    saved = inputs_ref[rows_of(mp), :].astype(F32)
    rstd = lax.rsqrt(jnp.mean(saved * saved, axis=-1, keepdims=True) + 1e-06)
    input_gradient, part = norm_reverse_pass(
        outgrad_ref[rows_of(mp), :], normed_grad, saved * rstd, rstd, gain_ref[...]
    )
    gi_buf[...] = input_gradient.astype(BF16)
    gain_slots[mp] = jnp.broadcast_to(part[None, :], gain_slots.shape[1:])
    gi_keep.start()
    for i in others:
        gi_copy(i).start()
        slot_copy(i).start()

    def count(array):
        return pieces if array < 3 else per_chunk

    for array in range(4):

        def pass_on(piece, carry, array=array):
            for kind in (0, 1):
                own(kind, array, piece).wait_recv()
                forward(kind, array, piece).start()
            return carry

        lax.fori_loop(0, count(array), pass_on, 0)
        if array == 0:
            for i in others:
                slot_copy(i).wait()
            part = gain_slots[0]
            for i in others:
                part += gain_slots[i]
            gain_seqs[me] = part.astype(BF16).astype(F32)
            for mask in (1, 2, 3):
                seq_copy(mask).start()
    for array in range(4):

        def finish(piece, carry, array=array):
            for kind in (0, 1):
                own(kind, array, piece).wait_send()
                forward(kind, array, piece).wait()
            keep(array, piece).wait()
            return carry

        lax.fori_loop(0, count(array), finish, 0)
    for mask in (1, 2, 3):
        seq_copy(mask).wait()
    gain_out[...] = (gain_seqs[0] + gain_seqs[1]) + (gain_seqs[2] + gain_seqs[3])
    for i in others:
        total_copy(i).wait_send()
        gi_copy(i).wait()
    gi_keep.wait()


def fused_shards(
    n_mp,
    inputs,
    norm_gain_vector,
    query_saved,
    key_saved,
    value_saved,
    w_query,
    w_key,
    w_value,
    w_out,
    output_gradient,
):
    widened_rows = inputs.astype(F32)
    reciprocal_deviation = lax.rsqrt(
        jnp.mean(widened_rows * widened_rows, axis=-1, keepdims=True) + 1e-06
    )
    normalized_rows = (widened_rows * reciprocal_deviation * norm_gain_vector).astype(BF16)
    length, width = query_saved.shape
    features = normalized_rows.shape[1]
    steps = width // HD
    per_chunk = steps // N_DP
    rows = jnp.stack([normalized_rows.T, output_gradient.T])
    vmem, hbm = pl.BlockSpec(memory_space=pltpu.VMEM), pl.BlockSpec(memory_space=pl.ANY)
    dma = pltpu.SemaphoreType.DMA
    grads, att, gathered, total = pl.pallas_call(
        functools.partial(attention_kernel, n_mp),
        out_shape=(
            jax.ShapeDtypeStruct((per_chunk, N_DP, length, 3 * HD), BF16),
            jax.ShapeDtypeStruct((per_chunk, N_DP, HD, length), BF16),
            jax.ShapeDtypeStruct((2, N_DP, features, length), BF16),
            jax.ShapeDtypeStruct((length, features), BF16),
        ),
        in_specs=[hbm] * 7 + [vmem],
        out_specs=(hbm, hbm, hbm, vmem),
        scratch_shapes=[pltpu.VMEM((length, width), BF16)] * 3
        + [pltpu.VMEM((features, width), BF16)] * 3
        + [pltpu.VMEM((width, features), BF16)]
        + [
            pltpu.VMEM((steps, length, 3 * HD), BF16),
            pltpu.VMEM((steps, HD, length), BF16),
            pltpu.VMEM((length, features), F32),
            dma((2, steps)),
            dma((2, steps)),
            dma((3 * n_mp,)),
            dma((3 * n_mp,)),
            dma((2,)),
            dma((7,)),
        ],
        compiler_params=pltpu.CompilerParams(
            collective_id=0, has_side_effects=True, vmem_limit_bytes=56 * 2**20
        ),
        cost_estimate=pl.CostEstimate(
            flops=30 * length * width * features, bytes_accessed=40 * 2**20, transcendentals=0
        ),
    )(query_saved, key_saved, value_saved, w_query, w_key, w_value, w_out, rows)
    pieces = 4
    outs = pl.pallas_call(
        functools.partial(weight_kernel, n_mp),
        out_shape=(jax.ShapeDtypeStruct((features, width), BF16),) * 3
        + (
            jax.ShapeDtypeStruct((width, features), BF16),
            jax.ShapeDtypeStruct((length, features), BF16),
            jax.ShapeDtypeStruct((8, features), F32),
        ),
        in_specs=[vmem, hbm, hbm, vmem, vmem, vmem, vmem],
        out_specs=(hbm,) * 5 + (vmem,),
        scratch_shapes=[
            pltpu.VMEM(att.shape, BF16),
            pltpu.VMEM(gathered.shape, BF16),
            pltpu.VMEM((3, pieces, features // pieces, per_chunk * HD), BF16),
            pltpu.VMEM((per_chunk, HD, features), BF16),
            pltpu.VMEM((n_mp, length // n_mp, features), BF16),
            pltpu.VMEM((length // n_mp, features), BF16),
            pltpu.VMEM((n_mp, 8, features), F32),
            pltpu.VMEM((N_DP, 8, features), F32),
            dma((4, 4, max(pieces, per_chunk))),
            dma((4, 4, max(pieces, per_chunk))),
            dma((4, max(pieces, per_chunk))),
            dma((3,)),
        ]
        + [dma((n_mp,))] * 6
        + [dma((N_DP,))] * 2,
        compiler_params=pltpu.CompilerParams(
            collective_id=1, has_side_effects=True, vmem_limit_bytes=48 * 2**20
        ),
        cost_estimate=pl.CostEstimate(
            flops=200 * length * width * features, bytes_accessed=200 * 2**20, transcendentals=0
        ),
    )(grads, att, gathered, total, inputs, output_gradient, norm_gain_vector.reshape(1, features))
    *weights, grad_inputs, sum_gain = outs
    return (grad_inputs, *weights, sum_gain[0])


def fits(mesh, arguments):
    length, width = arguments[2].shape
    n_dp, n_mp = mesh.shape["dp"], mesh.shape["mp"]
    return (
        n_dp == N_DP
        and n_mp == 8
        and width % (n_mp * N_DP * HD) == 0
        and width <= 2048 * n_mp
        and length == 512 * n_dp
        and arguments[0].shape[1] == 1024
    )


def solution(mesh):
    def whole(*arguments):
        return jax.shard_map(
            functools.partial(fused_shards, mesh.shape["mp"]) if fits(mesh, arguments) else shards,
            mesh=mesh,
            in_specs=(
                P("dp", None),
                P(),
                P("dp", "mp"),
                P("dp", "mp"),
                P("dp", "mp"),
                P(None, "mp"),
                P(None, "mp"),
                P(None, "mp"),
                P("mp", None),
                P("dp", None),
            ),
            out_specs=(
                P("dp", None), P(None, "mp"), P(None, "mp"), P(None, "mp"), P("mp", None), P(),
            ),
            check_vma=False,
        )(*arguments)

    return whole
```

```python
import functools

import jax
import jax.numpy as jnp
from jax import lax
from jax.experimental import pallas as pl
from jax.experimental.pallas import tpu as pltpu
from jax.sharding import PartitionSpec as P

HD = 128
N_DP = 4
MESH = pl.DeviceIdType.MESH
F32 = jnp.float32
BF16 = jnp.bfloat16


def norm_reverse_pass(
    gradient_rows, normalized_gradient, unit_input_rows, reciprocal_deviation, norm_gain_vector
):
    scaled_gradient = normalized_gradient * norm_gain_vector
    inner_product = jnp.mean(scaled_gradient * unit_input_rows, axis=-1, keepdims=True)
    input_gradient = gradient_rows.astype(jnp.float32) + reciprocal_deviation * (
        scaled_gradient - unit_input_rows * inner_product
    )
    return (input_gradient, jnp.sum(normalized_gradient * unit_input_rows, axis=0))


def shards(
    inputs,
    norm_gain_vector,
    query_saved,
    key_saved,
    value_saved,
    w_query,
    w_key,
    w_value,
    w_out,
    output_gradient,
):
    single_float_type = jnp.float32
    brain_float_half = jnp.bfloat16
    length = inputs.shape[0]
    width = query_saved.shape[1]
    heads = width // HD
    widened_rows = inputs.astype(single_float_type)
    reciprocal_deviation = lax.rsqrt(
        jnp.mean(widened_rows * widened_rows, axis=-1, keepdims=True) + 1e-06
    )
    unit_input_rows = widened_rows * reciprocal_deviation
    normalized_rows = (unit_input_rows * norm_gain_vector).astype(brain_float_half)
    query = query_saved.reshape(length, heads, HD)
    keys = key_saved.reshape(length, heads, HD)
    values = value_saved.reshape(length, heads, HD)
    scores = jnp.einsum("qhd,khd->hqk", query, keys, preferred_element_type=single_float_type)
    probs = jax.nn.softmax(scores, axis=-1)
    probs_low = probs.astype(brain_float_half)
    attended = (
        jnp.einsum("hqk,khd->qhd", probs_low, values, preferred_element_type=single_float_type)
        .astype(brain_float_half)
        .reshape(length, width)
    )
    grad_att = jnp.einsum(
        "td,id->ti", output_gradient, w_out, preferred_element_type=single_float_type
    ).astype(brain_float_half)
    part_out = jnp.einsum(
        "ti,td->id", attended, output_gradient, preferred_element_type=single_float_type
    )
    grad_att3 = grad_att.reshape(length, heads, HD)
    grad_val = (
        jnp.einsum("hqk,qhd->khd", probs_low, grad_att3, preferred_element_type=single_float_type)
        .astype(brain_float_half)
        .reshape(length, width)
    )
    grad_prob = jnp.einsum(
        "qhd,khd->hqk", grad_att3, values, preferred_element_type=single_float_type
    )
    delta = jnp.sum(probs * grad_prob, axis=-1, keepdims=True)
    grad_score = (probs * (grad_prob - delta)).astype(brain_float_half)
    grad_query = (
        jnp.einsum("hqk,khd->qhd", grad_score, keys, preferred_element_type=single_float_type)
        .astype(brain_float_half)
        .reshape(length, width)
    )
    grad_key = (
        jnp.einsum("hqk,qhd->khd", grad_score, query, preferred_element_type=single_float_type)
        .astype(brain_float_half)
        .reshape(length, width)
    )
    part_query = jnp.einsum(
        "td,ti->di", normalized_rows, grad_query, preferred_element_type=single_float_type
    )
    part_key = jnp.einsum(
        "td,ti->di", normalized_rows, grad_key, preferred_element_type=single_float_type
    )
    part_value = jnp.einsum(
        "td,ti->di", normalized_rows, grad_val, preferred_element_type=single_float_type
    )
    total = jnp.einsum("ti,di->td", grad_query, w_query, preferred_element_type=single_float_type)
    total = total + jnp.einsum(
        "ti,di->td", grad_key, w_key, preferred_element_type=single_float_type
    )
    normalized_gradient = lax.psum(
        (
            total
            + jnp.einsum("ti,di->td", grad_val, w_value, preferred_element_type=single_float_type)
        ).astype(jnp.bfloat16),
        "mp",
    ).astype(jnp.float32)
    input_gradient, partial_gain = norm_reverse_pass(
        output_gradient,
        normalized_gradient,
        unit_input_rows,
        reciprocal_deviation,
        norm_gain_vector,
    )
    grad_inputs = input_gradient.astype(brain_float_half)
    sum_query, sum_key, sum_value, sum_out, sum_gain = (
        lax.psum(part_query.astype(jnp.bfloat16), "dp").astype(jnp.float32),
        lax.psum(part_key.astype(jnp.bfloat16), "dp").astype(jnp.float32),
        lax.psum(part_value.astype(jnp.bfloat16), "dp").astype(jnp.float32),
        lax.psum(part_out.astype(jnp.bfloat16), "dp").astype(jnp.float32),
        lax.psum(partial_gain.astype(jnp.bfloat16), "dp").astype(jnp.float32),
    )
    return (
        grad_inputs,
        sum_query.astype(brain_float_half),
        sum_key.astype(brain_float_half),
        sum_value.astype(brain_float_half),
        sum_out.astype(brain_float_half),
        sum_gain,
    )


def dot_nn(a, b):
    return lax.dot_general(a, b, (((1,), (0,)), ((), ())), preferred_element_type=F32)


def dot_nt(a, b):
    return lax.dot_general(a, b, (((1,), (1,)), ((), ())), preferred_element_type=F32)


def dot_tn(a, b):
    return lax.dot_general(a, b, (((0,), (0,)), ((), ())), preferred_element_type=F32)


def flipped(me, mask):
    x, y = me % 2, me // 2
    bx, by = mask % 2, mask // 2
    return (y + by * (1 - 2 * y)) * 2 + x + bx * (1 - 2 * x)


def greet(partners):
    barrier = pltpu.get_barrier_semaphore()
    for partner in partners:
        pl.semaphore_signal(barrier, inc=1, device_id=partner, device_id_type=MESH)
    pl.semaphore_wait(barrier, len(partners))


def fused_kernel(
    n_mp,
    q_hbm, k_hbm, v_hbm, wq_hbm, wk_hbm, wv_hbm, wo_hbm,
    rows_ref, inputs_ref, outgrad_ref, gain_ref,
    gathered_out, gq_out, gk_out, gv_out, go_out, gi_out, gain_out,
    q_ref, k_ref, v_ref, wq_ref, wk_ref, wv_ref, wo_ref,
    grads_buf, att_buf, total, total_ref, grads_ref, att_ref,
    landing, gi_buf, gain_slots, gain_seqs,
    a2a_send, a2a_recv, gather_send, gather_recv, local_sem, load_sem, unpack_sem,
    send_sem, recv_sem, keep_sem,
    total_send, total_recv, gi_send, gi_recv, slot_send, slot_recv, seq_send, seq_recv,
):
    me, mp = lax.axis_index("dp"), lax.axis_index("mp")
    parts = n_mp // 2
    core, z = mp % 2, mp // 2
    other_core = (me, mp + 1 - 2 * core)
    loads = [
        pltpu.make_async_copy(src, dst, load_sem.at[i])
        for i, (src, dst) in enumerate(
            (
                (q_hbm, q_ref), (k_hbm, k_ref), (v_hbm, v_ref), (wo_hbm, wo_ref),
                (wq_hbm, wq_ref), (wk_hbm, wk_ref), (wv_hbm, wv_ref),
            )
        )
    ]
    for load in loads:
        load.start()

    def along(j):
        return (me, (z + j) % parts * 2 + core)

    greet(
        [(flipped(me, mask), mp) for mask in (1, 2, 3)]
        + [(me, (mp + i) % n_mp) for i in range(1, n_mp)]
    )
    depth = rows_ref.shape[1] // parts
    steps = grads_buf.shape[0]

    def gather_copy(slot, src, array, owner, part, target):
        rows = pl.ds(pl.multiple_of(part * depth, depth), depth)
        return pltpu.make_async_remote_copy(
            src_ref=src.at[array, rows] if src is rows_ref else src.at[array, owner, rows],
            dst_ref=gathered_out.at[array, owner, rows],
            send_sem=gather_send.at[slot],
            recv_sem=gather_recv.at[slot],
            device_id=target,
            device_id_type=MESH,
        )

    def spread(mask):
        return gather_copy(mask - 1, rows_ref, core, me, z, (flipped(me, mask), mp))

    def along_z(mask, j):
        return gather_copy(
            3 * j + mask - 1, gathered_out, core, flipped(me, mask), z, along(j)
        )

    def across(mask, j):
        return gather_copy(
            3 * (parts + j) + mask - 1, gathered_out, core, flipped(me, mask),
            (z - j + parts) % parts, other_core,
        )

    def own_rows(array):
        return pltpu.make_async_copy(
            rows_ref.at[array], gathered_out.at[array, me], local_sem.at[array]
        )

    for mask in (1, 2, 3):
        spread(mask).start()
    own_rows(0).start()
    own_rows(1).start()

    def place(step):
        return step // N_DP, flipped(me, (step % N_DP + 1) % N_DP)

    def remote(step, kinds=(0, 1)):
        k, target = place(step)
        return [
            pltpu.make_async_remote_copy(
                src_ref=buf.at[step],
                dst_ref=out.at[k, me],
                send_sem=a2a_send.at[i, step],
                recv_sem=a2a_recv.at[i, step],
                device_id=(target, mp),
                device_id_type=MESH,
            )
            for i, (buf, out) in enumerate(((grads_buf, grads_ref), (att_buf, att_ref)))
            if i in kinds
        ]

    def local(step, kinds=(0, 1)):
        k, _ = place(step)
        return [
            pltpu.make_async_copy(buf.at[step], out.at[k, me], a2a_send.at[i, step])
            for i, (buf, out) in enumerate(((grads_buf, grads_ref), (att_buf, att_ref)))
            if i in kinds
        ]

    total[...] = jnp.zeros_like(total)
    for load in loads[:4]:
        load.wait()
    per_chunk = steps // N_DP

    def head_step(step, carry):
        k, target = place(step)
        cols = pl.ds(pl.multiple_of((target * per_chunk + k) * HD, HD), HD)
        query, keys, values = q_ref[:, cols], k_ref[:, cols], v_ref[:, cols]
        grad_att = dot_nn(wo_ref[cols, :], rows_ref[1]).astype(BF16)
        scores = dot_nt(keys, query)
        weights = jnp.exp(scores - jnp.max(scores, axis=0, keepdims=True))
        probs = weights * (1.0 / jnp.sum(weights, axis=0, keepdims=True))
        probs_low = probs.astype(BF16)
        att_buf[step] = dot_tn(values, probs_low).astype(BF16)
        grad_val = dot_nt(probs_low, grad_att).astype(BF16)
        grad_prob = dot_nn(values, grad_att)
        delta = jnp.sum(probs * grad_prob, axis=0, keepdims=True)
        grad_score = (probs * (grad_prob - delta)).astype(BF16)
        grad_query = jnp.transpose(dot_tn(keys, grad_score)).astype(BF16)
        grad_key = dot_nn(grad_score, query).astype(BF16)
        grads = jnp.concatenate([grad_query, grad_key, grad_val], axis=1)
        grads_buf[step] = grads

        @pl.when(step % N_DP != N_DP - 1)
        def _():
            for copy in remote(step):
                copy.start()

        @pl.when(step % N_DP == N_DP - 1)
        def _():
            for copy in local(step):
                copy.start()

        @pl.when(step == 0)
        def _():
            for load in loads[4:]:
                load.wait()

        projections = jnp.concatenate([wq_ref[:, cols], wk_ref[:, cols], wv_ref[:, cols]], axis=1)
        total[...] += dot_nt(grads, projections)
        return carry

    lax.fori_loop(0, N_DP, head_step, 0)
    for mask in (1, 2, 3):
        spread(mask).wait_recv()
        for j in range(1, parts):
            along_z(mask, j).start()
        across(mask, 0).start()
    lax.fori_loop(N_DP, steps, head_step, 0)
    total_ref[...] = total[...].astype(BF16)

    def ahead(i):
        return (mp + i) % n_mp

    share = total_ref.shape[0] // n_mp

    def rows_of(index):
        return pl.ds(pl.multiple_of(index * share, share), share)

    def total_copy(i):
        return pltpu.make_async_remote_copy(
            src_ref=total_ref.at[rows_of(ahead(i))],
            dst_ref=landing.at[i],
            send_sem=total_send.at[i],
            recv_sem=total_recv.at[i],
            device_id=(me, ahead(i)),
            device_id_type=MESH,
        )

    def gi_copy(i):
        return pltpu.make_async_remote_copy(
            src_ref=gi_buf,
            dst_ref=gi_out.at[rows_of(mp)],
            send_sem=gi_send.at[i],
            recv_sem=gi_recv.at[i],
            device_id=(me, ahead(i)),
            device_id_type=MESH,
        )

    def slot_copy(i):
        return pltpu.make_async_remote_copy(
            src_ref=gain_slots.at[mp],
            dst_ref=gain_slots.at[mp],
            send_sem=slot_send.at[i],
            recv_sem=slot_recv.at[i],
            device_id=(me, ahead(i)),
            device_id_type=MESH,
        )

    def seq_copy(mask):
        return pltpu.make_async_remote_copy(
            src_ref=gain_seqs.at[me],
            dst_ref=gain_seqs.at[me],
            send_sem=seq_send.at[mask],
            recv_sem=seq_recv.at[mask],
            device_id=(flipped(me, mask), mp),
            device_id_type=MESH,
        )

    gi_keep = pltpu.make_async_copy(gi_buf, gi_out.at[rows_of(mp)], gi_send.at[0])
    others = range(1, n_mp)
    for i in others:
        total_copy(i).start()
    for j in range(1, parts):
        for mask in (1, 2, 3):
            along_z(mask, j).wait_recv()
            across(mask, j).start()
    own_rows(0).wait()
    own_rows(1).wait()
    for j in range(parts):
        for mask in (1, 2, 3):
            across(mask, j).wait_recv()
    length = rows_ref.shape[2]
    unpacks = [
        pltpu.make_async_copy(
            gathered_out.at[array, owner],
            ref.at[:, owner * length : (owner + 1) * length],
            unpack_sem.at[array, owner],
        )
        for array, ref in ((1, wk_ref), (0, wq_ref))
        for owner in range(N_DP)
    ]
    for unpack in unpacks:
        unpack.start()

    peer_x, peer_y = flipped(me, 1), flipped(me, 2)
    pieces = 4
    height, width = rows_ref.shape[1] // pieces, per_chunk * HD
    outs = (gq_out, gk_out, gv_out, go_out)

    def spot(array, piece, owner, part=None):
        if array < 3:
            first, size = piece * height, height
            cols = pl.ds(pl.multiple_of(owner * width, width), width)
        else:
            first, size = (owner * per_chunk + piece) * HD, HD
            cols = slice(None)
        if part is not None:
            size = size // 2
            first = first + part * size
        return outs[array].at[pl.ds(pl.multiple_of(first, size), size), cols]

    def staged(array, piece):
        if array == 3:
            return wo_ref.at[pl.ds(pl.multiple_of(piece * HD, HD), HD)]
        across_rows = q_ref.shape[0] // height
        rows = pl.ds(pl.multiple_of(piece % across_rows * height, height), height)
        cols = pl.ds(pl.multiple_of(piece // across_rows * width, width), width)
        return (q_ref, k_ref, v_ref)[array].at[rows, cols]

    def copy_to(kind, array, piece, src, dst, peer):
        return pltpu.make_async_remote_copy(
            src_ref=src,
            dst_ref=dst,
            send_sem=send_sem.at[kind, array, piece],
            recv_sem=recv_sem.at[kind, array, piece],
            device_id=(peer, mp),
            device_id_type=MESH,
        )

    def own(kind, array, piece):
        return copy_to(
            kind, array, piece, staged(array, piece), spot(array, piece, me), (peer_x, peer_y)[kind]
        )

    def forward(kind, array, piece):
        block = spot(array, piece, (peer_x, peer_y)[kind], kind)
        return copy_to(2 + kind, array, piece, block, block, (peer_y, peer_x)[kind])

    def keep(array, piece):
        return pltpu.make_async_copy(
            staged(array, piece), spot(array, piece, me), keep_sem.at[array, piece]
        )

    def send(array, piece):
        own(0, array, piece).start()
        own(1, array, piece).start()
        keep(array, piece).start()

    def settle(step, i):
        @pl.when(step % N_DP != N_DP - 1)
        def _():
            remote(step, (i,))[0].wait_recv()

        @pl.when(step % N_DP == N_DP - 1)
        def _():
            local(step, (i,))[0].wait()

    def settle_step(i, step, carry):
        settle(step, i)
        return carry

    for unpack in unpacks[:N_DP]:
        unpack.wait()

    def tall_step(piece, carry):
        lax.fori_loop(
            piece * N_DP, (piece + 1) * N_DP, functools.partial(settle_step, 1), 0
        )
        acc = None
        for owner in range(N_DP):
            term = dot_nt(
                att_ref[piece, owner], wk_ref[:, owner * length : (owner + 1) * length]
            )
            acc = term if acc is None else acc + term
        staged(3, piece)[...] = acc.astype(BF16)
        send(3, piece)
        return carry

    lax.fori_loop(0, per_chunk, tall_step, 0)
    for unpack in unpacks[N_DP:]:
        unpack.wait()
    lax.fori_loop(0, steps, functools.partial(settle_step, 0), 0)
    for array in range(3):
        lanes = slice(array * HD, (array + 1) * HD)

        def wide_step(piece, carry, array=array, lanes=lanes):
            rows = pl.ds(pl.multiple_of(piece * height, height), height)
            acc = None
            for owner in range(N_DP):
                right = jnp.concatenate(
                    [grads_ref[k, owner, :, lanes] for k in range(per_chunk)], axis=1
                )
                term = dot_nn(wq_ref[rows, owner * length : (owner + 1) * length], right)
                acc = term if acc is None else acc + term
            staged(array, piece)[...] = acc.astype(BF16)
            send(array, piece)
            return carry

        lax.fori_loop(0, pieces, wide_step, 0)

    normed_grad = total_ref[rows_of(mp), :].astype(F32)
    for i in others:
        total_copy(i).wait_recv()
        normed_grad += landing[i].astype(F32)
    saved = inputs_ref[rows_of(mp), :].astype(F32)
    rstd = lax.rsqrt(jnp.mean(saved * saved, axis=-1, keepdims=True) + 1e-06)
    input_gradient, part = norm_reverse_pass(
        outgrad_ref[rows_of(mp), :], normed_grad, saved * rstd, rstd, gain_ref[...]
    )
    gi_buf[...] = input_gradient.astype(BF16)
    gain_slots[mp] = jnp.broadcast_to(part[None, :], gain_slots.shape[1:])
    gi_keep.start()
    for i in others:
        gi_copy(i).start()
        slot_copy(i).start()

    def count(array):
        return pieces if array < 3 else per_chunk

    for array in (3, 0, 1, 2):

        def pass_on(piece, carry, array=array):
            for kind in (0, 1):
                own(kind, array, piece).wait_recv()
                forward(kind, array, piece).start()
            return carry

        lax.fori_loop(0, count(array), pass_on, 0)
        if array == 3:
            for i in others:
                slot_copy(i).wait()
            part = gain_slots[0]
            for i in others:
                part += gain_slots[i]
            gain_seqs[me] = part.astype(BF16).astype(F32)
            for mask in (1, 2, 3):
                seq_copy(mask).start()
    for array in range(4):

        def finish(piece, carry, array=array):
            for kind in (0, 1):
                own(kind, array, piece).wait_send()
                forward(kind, array, piece).wait()
            keep(array, piece).wait()
            return carry

        lax.fori_loop(0, count(array), finish, 0)
    for mask in (1, 2, 3):
        seq_copy(mask).wait()
    gain_out[...] = (gain_seqs[0] + gain_seqs[1]) + (gain_seqs[2] + gain_seqs[3])
    for i in others:
        total_copy(i).wait_send()
        gi_copy(i).wait()
    gi_keep.wait()

    def drain(step, carry):
        @pl.when(step % N_DP != N_DP - 1)
        def _():
            for copy in remote(step):
                copy.wait_send()

        return carry

    lax.fori_loop(0, steps, drain, 0)
    for mask in (1, 2, 3):
        spread(mask).wait_send()
        for j in range(1, parts):
            along_z(mask, j).wait_send()
        for j in range(parts):
            across(mask, j).wait_send()


def place_kernel(count, *refs):
    sources, targets, stages = refs[:count], refs[count : 2 * count], refs[2 * count : 3 * count]
    read_sem, write_sem = refs[3 * count :]

    def copies(array, part):
        rows = sources[array].shape[0] // 4
        block = pl.ds(part * rows, rows)
        stage = stages[array].at[block]
        return (
            pltpu.make_async_copy(sources[array].at[block], stage, read_sem.at[array, part]),
            pltpu.make_async_copy(stage, targets[array].at[block], write_sem.at[array, part]),
        )

    pairs = [copies(array, part) for array in range(count) for part in range(4)]
    for read, _ in pairs:
        read.start()
    for read, write in pairs:
        read.wait()
        write.start()
    for _, write in pairs:
        write.wait()


def placed(arrays):
    hbm = pl.BlockSpec(memory_space=pl.ANY)
    count = len(arrays)
    return pl.pallas_call(
        functools.partial(place_kernel, count),
        out_shape=tuple(jax.ShapeDtypeStruct(a.shape, a.dtype) for a in arrays),
        in_specs=[hbm] * count,
        out_specs=(hbm,) * count,
        scratch_shapes=[pltpu.VMEM(a.shape, a.dtype) for a in arrays]
        + [pltpu.SemaphoreType.DMA((count, 4))] * 2,
        compiler_params=pltpu.CompilerParams(vmem_limit_bytes=60 * 2**20),
    )(*arrays)


def fused_shards(
    n_mp,
    inputs,
    norm_gain_vector,
    query_saved,
    key_saved,
    value_saved,
    w_query,
    w_key,
    w_value,
    w_out,
    output_gradient,
):
    widened_rows = inputs.astype(F32)
    reciprocal_deviation = lax.rsqrt(
        jnp.mean(widened_rows * widened_rows, axis=-1, keepdims=True) + 1e-06
    )
    normalized_rows = (widened_rows * reciprocal_deviation * norm_gain_vector).astype(BF16)
    length, width = query_saved.shape
    features = normalized_rows.shape[1]
    steps = width // HD
    per_chunk = steps // N_DP
    rows = jnp.stack([normalized_rows.T, output_gradient.T])
    vmem, hbm = pl.BlockSpec(memory_space=pltpu.VMEM), pl.BlockSpec(memory_space=pl.ANY)
    dma = pltpu.SemaphoreType.DMA
    pieces = max(4, per_chunk)
    _, *weights, grad_inputs, sum_gain = pl.pallas_call(
        functools.partial(fused_kernel, n_mp),
        out_shape=(jax.ShapeDtypeStruct((2, N_DP, features, length), BF16),)
        + (jax.ShapeDtypeStruct((features, width), BF16),) * 3
        + (
            jax.ShapeDtypeStruct((width, features), BF16),
            jax.ShapeDtypeStruct((length, features), BF16),
            jax.ShapeDtypeStruct((8, features), F32),
        ),
        in_specs=[hbm] * 7 + [vmem] * 4,
        out_specs=(hbm,) * 6 + (vmem,),
        scratch_shapes=[pltpu.VMEM((length, width), BF16)] * 3
        + [pltpu.VMEM((features, width), BF16)] * 3
        + [pltpu.VMEM((width, features), BF16)]
        + [
            pltpu.VMEM((steps, length, 3 * HD), BF16),
            pltpu.VMEM((steps, HD, length), BF16),
            pltpu.VMEM((length, features), F32),
            pltpu.VMEM((length, features), BF16),
            pltpu.VMEM((per_chunk, N_DP, length, 3 * HD), BF16),
            pltpu.VMEM((per_chunk, N_DP, HD, length), BF16),
            pltpu.VMEM((n_mp, length // n_mp, features), BF16),
            pltpu.VMEM((length // n_mp, features), BF16),
            pltpu.VMEM((n_mp, 8, features), F32),
            pltpu.VMEM((N_DP, 8, features), F32),
            dma((2, steps)),
            dma((2, steps)),
            dma((3 * n_mp,)),
            dma((3 * n_mp,)),
            dma((2,)),
            dma((7,)),
            dma((2, N_DP)),
            dma((4, 4, pieces)),
            dma((4, 4, pieces)),
            dma((4, pieces)),
        ]
        + [dma((n_mp,))] * 6
        + [dma((N_DP,))] * 2,
        compiler_params=pltpu.CompilerParams(
            collective_id=0, has_side_effects=True, vmem_limit_bytes=60 * 2**20
        ),
        cost_estimate=pl.CostEstimate(
            flops=46 * length * width * features, bytes_accessed=80 * 2**20, transcendentals=0
        ),
    )(
        query_saved, key_saved, value_saved, w_query, w_key, w_value, w_out,
        rows, inputs, output_gradient, norm_gain_vector.reshape(1, features),
    )
    return (*placed((grad_inputs, *weights)), sum_gain[0])


def fits(mesh, arguments):
    length, width = arguments[2].shape
    n_dp, n_mp = mesh.shape["dp"], mesh.shape["mp"]
    return (
        n_dp == N_DP
        and n_mp == 8
        and width % (n_mp * N_DP * HD) == 0
        and width == 2048 * n_mp
        and length == 512 * n_dp
        and arguments[0].shape[1] == 1024
    )


def solution(mesh):
    def whole(*arguments):
        return jax.shard_map(
            functools.partial(fused_shards, mesh.shape["mp"]) if fits(mesh, arguments) else shards,
            mesh=mesh,
            in_specs=(
                P("dp", None),
                P(),
                P("dp", "mp"),
                P("dp", "mp"),
                P("dp", "mp"),
                P(None, "mp"),
                P(None, "mp"),
                P(None, "mp"),
                P("mp", None),
                P("dp", None),
            ),
            out_specs=(
                P("dp", None), P(None, "mp"), P(None, "mp"), P(None, "mp"), P("mp", None), P(),
            ),
            check_vma=False,
        )(*arguments)

    return whole
```
